32 devices in a mesh: groups: 2 (over y), aperture: 4 (over z), range: 2 (over x), beam: 2 (over core).
Axes of the slice: x: 2, y: 2, z: 4, core: 2. Of those that a mesh axis runs over, the one named last changes fastest.
Arguments:
- polar: bfloat16 [8, 256, 128, 256], P(('groups', 'range', 'beam'), 'aperture'), parts along dimension 0, may hold values from -6 to 6
- route: int32 [8, 256, 1], P(('groups', 'range', 'beam'), 'aperture'), parts along dimension 0, may hold values from 0 to 7; in each aligned block of 64 rows (0 to 63, 64 to 127, ..., all dimensions but the last counted through in order) at most 16 rows name the same one
- kind: int32 [8, 256], P(('groups', 'range', 'beam'), 'aperture'), parts along dimension 0, may hold values from 0 to 7
- filt: bfloat16 [8, 128, 256], P(('groups', 'range', 'beam')), parts along dimension 0
- interp_angle: bfloat16 [8, 128, 256], replicated
- interp_range: bfloat16 [8, 128, 256], replicated
- twiddle: float32 [8, 128], P('aperture'), may hold values from -3.140625 to 3.140625
Outputs:
- next_section: float32 [8, 8, 128, 256], P(('groups', 'range', 'beam'), 'aperture'), parts along dimension 0
The draws below stay inside these ranges and needn't reach their ends.
There are 2 independent parts, one for each index of `groups`. The reference program is written for one: setup_inputs(seed, part) draws one part's arguments, and reference() takes and returns one part's arrays. A program takes and returns all parts, laid end to end along the dimension named above; an argument that names none is the same for every part. Nothing has to cross between parts.
Inputs may be any that keep to these rules, and one draw needn't show every extreme that they name: `route`: among the 64 blocks of one slab held by one device (aligned runs of 64 blocks), no tile is named more than 16 times, a bound that some block reaches.
All inputs are finite; a program needn't handle non-finite values.
Results may differ from the reference program's by a relative error of at most 0.004.
Values may be sent and summed in bfloat16 or wider, within the bound.
A program may use at most 192 MiB of HBM per device.

```python
import math
import jax
import jax.numpy as jnp
import numpy as np
from jax import lax

SIDE = 128
NKERN = 8
BLK_DEV = 64
SLABS = 4
BLOCKS = 256
TILES = 8
CAP = 16


def assemble(noise):
    spread = 0.5 / math.sqrt(SIDE)
    eye = jnp.eye(SIDE, dtype=jnp.float32)
    real = eye[None] + noise[:, 0] * spread
    imag = noise[:, 1] * spread
    return jnp.concatenate([real, imag], axis=-1).astype(jnp.bfloat16)


def draw_filt(key, part):
    key = jax.random.fold_in(key, 1)
    noise = jax.random.normal(key, (SLABS, 2, SIDE, SIDE), jnp.float32)
    return assemble(noise)


def draw_interp_angle(key, part):
    key = jax.random.fold_in(key, 2)
    noise = jax.random.normal(key, (NKERN, 2, SIDE, SIDE), jnp.float32)
    return assemble(noise)


def draw_interp_range(key, part):
    key = jax.random.fold_in(key, 3)
    noise = jax.random.normal(key, (NKERN, 2, SIDE, SIDE), jnp.float32)
    return assemble(noise)


def plant(entries, own_key, least, top_value):
    extent = entries.shape
    place = [jax.random.randint(jax.random.fold_in(own_key, axis), (), 0, extent[axis]) for axis in range(len(extent))]
    entries = entries.at[tuple(place)].set(least)
    longest = extent.index(max(extent))
    place[longest] = (place[longest] + 1) % extent[longest]
    return entries.at[tuple(place)].set(top_value)


def shard_levels(own_key, shape, pieces, low, largest):
    gain, own = 1.0, jax.random.fold_in(own_key, 6)
    for position, blocks in pieces:
        heights = jnp.exp(jax.random.uniform(jax.random.fold_in(own, position), (blocks,), jnp.float32, low / len(pieces), largest / len(pieces)))
        gain = gain * jnp.repeat(heights, shape[position] // blocks).reshape([-1 if axis == position else 1 for axis in range(len(shape))])
    return gain


def assign_block(rng, own, number, rows, count, top, bound, lean):
    ranking = jax.random.permutation(rng, count)
    packed, usual = portions_of(count, rows * top, bound, lean, True), portions_of(count, rows * top, bound, lean, False)
    places = jnp.arange(count)

    def named(tallies, rotation):
        used = int((tallies > 0).sum())
        fixed = max(1, used // 4)
        shifted = fixed + (places - fixed + rotation * (used - fixed)) % max(1, count - fixed)
        return jnp.zeros((count,), jnp.int32).at[ranking[jnp.where(places < fixed, places, shifted)]].set(jnp.asarray(tallies, jnp.int32))

    tallies = jnp.where(number % 4 == 0, named(packed, number // 4), named(usual, number - number // 4 - 1))
    mixed = jax.random.permutation(jax.random.fold_in(own, 3), count)
    source_of, receiver = mixed[0:count // 2 * 2:2], mixed[1:count // 2 * 2:2]
    margin = jnp.minimum(tallies[source_of] - 1, bound - tallies[receiver]) // 2
    margin = jnp.where((source_of == ranking[0]) | (receiver == ranking[0]) | (tallies[receiver] == 0), 0, jnp.maximum(margin, 0))
    shifted = jax.random.randint(jax.random.fold_in(own, 4), (count // 2,), 0, 1 << 20) % (margin + 1)
    tallies = tallies.at[source_of].add(-shifted).at[receiver].add(shifted)
    labels = jnp.searchsorted(jnp.cumsum(tallies), jnp.arange(rows * top), side="right").astype(jnp.int32)
    grid = labels.reshape(top, rows).T
    grid = grid[jax.random.permutation(jax.random.fold_in(own, 1), rows)]
    rotation = jax.random.randint(jax.random.fold_in(own, 2), (rows, 1), 0, top)
    return jnp.take_along_axis(grid, (jnp.arange(top)[None, :] + rotation) % top, axis=1)


def portions_of(amount, total, limit, slope, full):
    loads = [(1 << 20) // math.isqrt(grade ** slope) + 1 for grade in range(1, amount + 1)]
    largest = limit if full else min(limit, max(-(-total // amount), total * loads[0] // sum(loads)))
    least = 1 if total - largest >= amount - 1 else 0
    counts, spare = [largest] + [least] * (amount - 1), total - largest - least * (amount - 1)
    while spare > 0:
        candidates = [i for i in range(1, amount) if counts[i] < largest] or [i for i in range(1, amount) if counts[i] < limit]
        whole, remaining = sum([loads[i] for i in candidates]), spare
        for i in candidates:
            more = min(limit - counts[i], max(1, remaining * loads[i] // whole), spare)
            counts[i] = counts[i] + more
            spare = spare - more
    return np.array(counts)


def scatter_about(key, shape, scale, most, split=(), kind=jnp.bfloat16):
    drawn = scale * jax.random.normal(key, shape, jnp.float32)
    if split:
        drawn = drawn * shard_levels(key, shape, split, -0.22, 0.18)
    return jnp.clip(drawn, -most, most).astype(kind)


def setup_inputs(seed: int = 0, part: int = 0) -> dict:
    splits = jax.random.split(jax.random.key(seed), 8)
    own_keys = jax.random.split(jax.random.fold_in(splits[7], part), 8)
    polar = scatter_about(own_keys[0], (SLABS, BLOCKS, SIDE, 2 * SIDE), 1.0, 6.0, ((0, 4), (1, 4)))
    route_keys = jax.random.split(jax.random.fold_in(own_keys[1], 1), SLABS * BLOCKS // BLK_DEV)
    route_turns = jax.random.permutation(jax.random.fold_in(own_keys[1], 3), SLABS * BLOCKS // BLK_DEV)
    route = jax.vmap(lambda own, number: assign_block(jax.random.fold_in(own_keys[1], 2), own, number, BLK_DEV, TILES, 1, CAP, 2))(route_keys, route_turns).reshape((SLABS, BLOCKS, 1))
    kind = plant(jax.random.randint(own_keys[2], (SLABS, BLOCKS), 0, NKERN), jax.random.fold_in(own_keys[2], 1), 0, NKERN - 1).astype(jnp.int32)
    filt = draw_filt(jax.random.fold_in(jax.random.fold_in(splits[7], part), 71), part)
    interp_angle = draw_interp_angle(jax.random.fold_in(splits[7], 71), part)
    interp_range = draw_interp_range(jax.random.fold_in(splits[7], 71), part)
    twiddle = jnp.clip(jax.random.uniform(splits[6], (TILES, SIDE), jnp.float32, -3.140625, 3.140625), -3.140625, 3.140625)
    return dict(polar=polar, route=route, kind=kind, filt=filt, interp_angle=interp_angle, interp_range=interp_range, twiddle=twiddle)


def expand(matrix):
    width = matrix.shape[-2]
    real = matrix[..., :width]
    imag = matrix[..., width:]
    top = jnp.concatenate([real, imag], axis=-1)
    bottom = jnp.concatenate([-imag, real], axis=-1)
    return jnp.concatenate([top, bottom], axis=-2)


def compress(blocks, hmat):
    count, width, double = blocks.shape
    flat = jnp.dot(blocks.reshape(count * width, double), hmat, preferred_element_type=jnp.float32)
    return flat.reshape(count, width, double).astype(jnp.bfloat16)


def interpolate(comp, kinds, table_angle, table_range):
    width = comp.shape[1]
    left = table_angle[kinds].astype(jnp.float32)
    data = comp.astype(jnp.float32)
    prod_re = jnp.einsum("bij,bjk->bik", left[..., :width], data)
    prod_im = jnp.einsum("bij,bjk->bik", left[..., width:], data)
    ang_re = prod_re[..., :width] - prod_im[..., width:]
    ang_im = prod_re[..., width:] + prod_im[..., :width]
    angular = jnp.concatenate([ang_re, ang_im], axis=-1).astype(jnp.bfloat16)
    right = expand(table_range[kinds]).astype(jnp.float32)
    return jnp.einsum("bij,bjk->bik", angular.astype(jnp.float32), right)


def reference(polar, route, kind, filt, interp_angle, interp_range, twiddle):
    per_slab = BLOCKS // BLK_DEV
    count = SLABS * per_slab
    blocks = polar.reshape(count, BLK_DEV, SIDE, 2 * SIDE)
    dest = route.reshape(count, BLK_DEV).astype(jnp.int32)
    kinds = kind.reshape(count, BLK_DEV).astype(jnp.int32)

    def step(image, items):
        index, part, where, which = items
        slab = (index // per_slab).astype(jnp.int32)
        hmat = expand(filt[slab])
        comp = compress(part, hmat)
        contrib = interpolate(comp, which, interp_angle, interp_range)
        image = image.at[slab * TILES + where].add(contrib)
        return image, None

    image = jnp.zeros((SLABS * TILES, SIDE, 2 * SIDE), jnp.float32)
    image, _ = lax.scan(step, image, (jnp.arange(count, dtype=jnp.int32), blocks, dest, kinds))
    image = image.reshape(SLABS // 2, 2, TILES, SIDE, 2 * SIDE)
    even = image[:, 0]
    odd = image[:, 1]
    cos_part = jnp.cos(twiddle)[None, :, None, :]
    sin_part = jnp.sin(twiddle)[None, :, None, :]
    odd_re = odd[..., :SIDE]
    odd_im = odd[..., SIDE:]
    rotated = jnp.concatenate([cos_part * odd_re - sin_part * odd_im, cos_part * odd_im + sin_part * odd_re], axis=-1)
    merged = jnp.stack([even + rotated, even - rotated], axis=1)
    return merged.reshape(SLABS, TILES, SIDE, 2 * SIDE)
```

```python
import functools

import jax
import jax.numpy as jnp
from jax import lax
from jax.experimental import pallas as pl
from jax.experimental.pallas import tpu as pltpu
from jax.sharding import PartitionSpec as P

MESH = pl.DeviceIdType.MESH
CHUNKS = 8
PIECES = 4
GROUP = 2


def expand(matrix, width):
    real, imag = matrix[:, :width], matrix[:, width:]
    return jnp.concatenate(
        [jnp.concatenate([real, imag], axis=1), jnp.concatenate([-imag, real], axis=1)], axis=0
    )


def angle_kernel(
    nkern, route, kind, filt_hbm, angle_hbm, rng_hbm, polar, y, ghi, glo,
    filt, angle, rng, pbuf, table_sems, sems
):
    count, width, double = pbuf.shape
    per = count // CHUNKS

    def chunk_copy(c):
        part = pl.ds(c * per, per)
        return pltpu.make_async_copy(polar.at[part], pbuf.at[part], sems.at[c])

    tables = [
        pltpu.make_async_copy(src, dst, table_sems.at[i])
        for i, (src, dst) in enumerate(((filt_hbm, filt), (rng_hbm, rng), (angle_hbm, angle)))
    ]
    for copy in tables:
        copy.start()
    for c in range(CHUNKS):
        chunk_copy(c).start()

    @pl.loop(0, y.shape[0])
    def _(cell):
        y[cell] = jnp.zeros((width, double), jnp.float32)

    tables[0].wait()
    tables[1].wait()

    @pl.loop(0, nkern)
    def _(k):
        g = jnp.dot(filt[...], expand(rng[k], width), preferred_element_type=jnp.float32)
        hi = g.astype(jnp.bfloat16)
        lo = (g - hi.astype(jnp.float32)).astype(jnp.bfloat16)
        rows = pl.ds(pl.multiple_of(k * double, double), double)
        ghi[rows, :] = expand(hi, width)
        glo[rows, :] = expand(lo, width)

    tables[2].wait()

    @pl.loop(0, CHUNKS)
    def _(c):
        chunk_copy(c).wait()

        @pl.loop(0, per // GROUP)
        def _(g):
            outs = []
            cells = []
            for u in range(GROUP):
                j = c * per + g * GROUP + u
                k = kind[j]
                cells.append(route[j] * nkern + k)
                outs.append(
                    jnp.dot(
                        angle[k], expand(pbuf[j], width), preferred_element_type=jnp.float32
                    )
                )
            for cell, out in zip(cells, outs):
                y[cell] += out


def merge_kernel(
    n, y, ghi, glo, twiddle, out, xcat, own, sbuf, rbuf_r, rbuf_l, pair,
    send_sem, recv_r, recv_l, pair_send, pair_recv,
):
    tile_dev, width, double = out.shape
    rows = tile_dev * width
    nkern = ghi.shape[0] // double
    piece = rows // PIECES
    z = lax.axis_index("aperture")
    b = lax.axis_index("beam")
    has_left = z > 0
    has_right = z < n - 1

    barrier = pltpu.get_barrier_semaphore()

    @pl.when(has_left)
    def _():
        pl.semaphore_signal(barrier, inc=1, device_id={"aperture": z - 1}, device_id_type=MESH)

    @pl.when(has_right)
    def _():
        pl.semaphore_signal(barrier, inc=1, device_id={"aperture": z + 1}, device_id_type=MESH)

    pl.semaphore_signal(barrier, inc=1, device_id={"beam": 1 - b}, device_id_type=MESH)

    ahead = n - 1 - z
    near = jnp.minimum(ahead, z)
    lead = jnp.maximum(ahead, z) - near

    def dest(i):
        first = jnp.where(ahead > z, n - 1 - i, i)
        j = i - lead
        gap = near - j // 2
        later = jnp.where(j % 2 == 0, z + gap, z - gap)
        return jnp.where(i < lead, first, later)

    def span(p):
        return pl.ds(p * piece, piece)

    def send_right(d, p):
        return pltpu.make_async_remote_copy(
            src_ref=sbuf.at[d, span(p)], dst_ref=rbuf_r.at[d, span(p)],
            send_sem=send_sem.at[d, p], recv_sem=recv_r.at[d, p],
            device_id={"aperture": z + 1}, device_id_type=MESH,
        )

    def send_left(d, p):
        return pltpu.make_async_remote_copy(
            src_ref=sbuf.at[d, span(p)], dst_ref=rbuf_l.at[d, span(p)],
            send_sem=send_sem.at[d, p], recv_sem=recv_l.at[d, p],
            device_id={"aperture": z - 1}, device_id_type=MESH,
        )

    def send_pair(p):
        return pltpu.make_async_remote_copy(
            src_ref=own.at[z, span(p)], dst_ref=pair.at[span(p)],
            send_sem=pair_send.at[p], recv_sem=pair_recv.at[p],
            device_id={"beam": 1 - b}, device_id_type=MESH,
        )

    @pl.loop(0, n)
    def _(i):
        d = dest(i)
        for t in range(tile_dev):
            for k in range(nkern):
                xcat[t * width:(t + 1) * width, k * double:(k + 1) * double] = y[
                    (d * tile_dev + t) * nkern + k
                ].astype(jnp.bfloat16)
        own[d] = jnp.dot(xcat[...], ghi[...], preferred_element_type=jnp.float32) + jnp.dot(
            xcat[...], glo[...], preferred_element_type=jnp.float32
        )

        @pl.when(i == 0)
        def _():
            links = has_left.astype(jnp.int32) + has_right.astype(jnp.int32) + 1
            pl.semaphore_wait(barrier, links)

        @pl.when(jnp.logical_and(z == 0, d > z))
        def _():
            sbuf[d] = own[d].astype(jnp.bfloat16)
            for p in range(PIECES):
                send_right(d, p).start()

        @pl.when(jnp.logical_and(z == n - 1, d < z))
        def _():
            sbuf[d] = own[d].astype(jnp.bfloat16)
            for p in range(PIECES):
                send_left(d, p).start()

    @pl.when(jnp.logical_and(has_left, has_right))
    def _():
        @pl.loop(0, n - 1)
        def _(i):
            d = dest(i)

            @pl.when(d > z)
            def _():
                for p in range(PIECES):
                    send_right(d, p).wait_recv()
                    part = own[d, span(p)] + rbuf_r[d, span(p)].astype(jnp.float32)
                    sbuf[d, span(p)] = part.astype(jnp.bfloat16)
                    send_right(d, p).start()

            @pl.when(d < z)
            def _():
                for p in range(PIECES):
                    send_left(d, p).wait_recv()
                    part = own[d, span(p)] + rbuf_l[d, span(p)].astype(jnp.float32)
                    sbuf[d, span(p)] = part.astype(jnp.bfloat16)
                    send_left(d, p).start()

    for p in range(PIECES):
        @pl.when(has_left)
        def _():
            send_right(z, p).wait_recv()
            own[z, span(p)] += rbuf_r[z, span(p)].astype(jnp.float32)

        @pl.when(has_right)
        def _():
            send_left(z, p).wait_recv()
            own[z, span(p)] += rbuf_l[z, span(p)].astype(jnp.float32)

        send_pair(p).start()

    cos_all, sin_all = jnp.cos(twiddle[...]), jnp.sin(twiddle[...])
    is_even = b == 0
    sign = jnp.where(is_even, 1.0, -1.0).astype(jnp.float32)
    for p in range(PIECES):
        send_pair(p).wait_recv()
        t, base = p * piece // width, p * piece % width
        mine, other = own[z, span(p)], pair[span(p)]
        even = jnp.where(is_even, mine, other)
        odd = jnp.where(is_even, other, mine)
        cos, sin = cos_all[t:t + 1], sin_all[t:t + 1]
        odd_re, odd_im = odd[:, :width], odd[:, width:]
        out[t, base:base + piece, :width] = even[:, :width] + sign * (cos * odd_re - sin * odd_im)
        out[t, base:base + piece, width:] = even[:, width:] + sign * (cos * odd_im + sin * odd_re)

    for p in range(PIECES):
        send_pair(p).wait_send()

    @pl.loop(0, n)
    def _(d):
        @pl.when(d != z)
        def _():
            for p in range(PIECES):
                send_right(d, p).wait_send()


def per_device(polar, route, kind, filt, interp_angle, interp_range, twiddle):
    n = lax.axis_size("aperture")
    tile_dev = twiddle.shape[0]
    tiles = tile_dev * n
    _, count, width, double = polar.shape
    nkern = interp_angle.shape[0]
    cells = tiles * nkern
    rows = tile_dev * width
    resident = cells * width * double * 4 <= 16 * 2**20
    held = pltpu.VMEM if resident else jax.ShapeDtypeStruct
    vmem = pl.BlockSpec(memory_space=pltpu.VMEM)
    smem = pl.BlockSpec(memory_space=pltpu.SMEM)
    y, ghi, glo = pl.pallas_call(
        functools.partial(angle_kernel, nkern),
        out_shape=[
            held((cells, width, double), jnp.float32),
            held((nkern * double, double), jnp.bfloat16),
            held((nkern * double, double), jnp.bfloat16),
        ],
        in_specs=[smem, smem] + [pl.BlockSpec(memory_space=pl.ANY)] * 4,
        out_specs=[vmem, vmem, vmem],
        scratch_shapes=[
            pltpu.VMEM((width, double), jnp.bfloat16),
            pltpu.VMEM((nkern, width, double), jnp.bfloat16),
            pltpu.VMEM((nkern, width, double), jnp.bfloat16),
            pltpu.VMEM((count, width, double), jnp.bfloat16),
            pltpu.SemaphoreType.DMA((3,)),
            pltpu.SemaphoreType.DMA((CHUNKS,)),
        ],
        compiler_params=pltpu.CompilerParams(vmem_limit_bytes=(24 if resident else 48) * 2**20),
        name="angle",
    )(
        *[
            pltpu.with_memory_space_constraint(v, pltpu.HBM)
            for v in (route[0, :, 0], kind[0], filt[0], interp_angle, interp_range, polar[0])
        ],
    )
    if resident:
        y, ghi, glo = [pltpu.with_memory_space_constraint(v, pltpu.VMEM) for v in (y, ghi, glo)]
    merged = pl.pallas_call(
        functools.partial(merge_kernel, n),
        out_shape=jax.ShapeDtypeStruct((tile_dev, width, double), jnp.float32),
        in_specs=[vmem, vmem, vmem, vmem],
        out_specs=vmem,
        scratch_shapes=[
            pltpu.VMEM((rows, nkern * double), jnp.bfloat16),
            pltpu.VMEM((n, rows, double), jnp.float32),
            pltpu.VMEM((n, rows, double), jnp.bfloat16),
            pltpu.VMEM((n, rows, double), jnp.bfloat16),
            pltpu.VMEM((n, rows, double), jnp.bfloat16),
            pltpu.VMEM((rows, double), jnp.float32),
            pltpu.SemaphoreType.DMA((n, PIECES)),
            pltpu.SemaphoreType.DMA((n, PIECES)),
            pltpu.SemaphoreType.DMA((n, PIECES)),
            pltpu.SemaphoreType.DMA((PIECES,)),
            pltpu.SemaphoreType.DMA((PIECES,)),
        ],
        compiler_params=pltpu.CompilerParams(
            vmem_limit_bytes=(24 if resident else 58) * 2**20, collective_id=0, has_side_effects=True
        ),
        name="merge",
    )(y, ghi, glo, pltpu.with_memory_space_constraint(twiddle, pltpu.HBM))
    return merged[None]


def solution(mesh):
    return jax.shard_map(
        per_device,
        mesh=mesh,
        in_specs=(
            P(("groups", "range", "beam"), "aperture", None, None),
            P(("groups", "range", "beam"), "aperture", None),
            P(("groups", "range", "beam"), "aperture"),
            P(("groups", "range", "beam"), None, None),
            P(),
            P(),
            P("aperture", None),
        ),
        out_specs=P(("groups", "range", "beam"), "aperture", None, None),
        check_vma=False,
    )
```

```python
import functools

import jax
import jax.numpy as jnp
from jax import lax
from jax.experimental import pallas as pl
from jax.experimental.pallas import tpu as pltpu
from jax.sharding import PartitionSpec as P

MESH = pl.DeviceIdType.MESH
CHUNKS = 2
PIECES = 8


def expand(matrix, width):
    real, imag = matrix[:, :width], matrix[:, width:]
    return jnp.concatenate(
        [jnp.concatenate([real, imag], axis=1), jnp.concatenate([-imag, real], axis=1)], axis=0
    )


def angle_kernel(
    nkern, route, kind, filt_hbm, angle_hbm, rng_hbm, polar, y, ghi, glo,
    filt, angle, rng, pbuf, table_sems, sems
):
    count, width, double = pbuf.shape
    per = count // CHUNKS

    def chunk_copy(c):
        part = pl.ds(c * per, per)
        return pltpu.make_async_copy(polar.at[part], pbuf.at[part], sems.at[c])

    tables = [
        pltpu.make_async_copy(src, dst, table_sems.at[i])
        for i, (src, dst) in enumerate(((filt_hbm, filt), (rng_hbm, rng), (angle_hbm, angle)))
    ]
    for copy in tables:
        copy.start()
    for c in range(CHUNKS):
        chunk_copy(c).start()

    tables[0].wait()
    tables[1].wait()

    products = [
        jnp.dot(filt[...], expand(rng[k], width), preferred_element_type=jnp.float32)
        for k in range(nkern)
    ]
    share = y.shape[0] // nkern
    for k, g in enumerate(products):
        for cell in range(k * share, (k + 1) * share):
            y[cell] = jnp.zeros((width, double), jnp.float32)
        hi = g.astype(jnp.bfloat16)
        lo = (g - hi.astype(jnp.float32)).astype(jnp.bfloat16)
        ghi[k * double:(k + 1) * double, :] = expand(hi, width)
        glo[k * double:(k + 1) * double, :] = expand(lo, width)

    tables[2].wait()

    @pl.loop(0, CHUNKS)
    def _(c):
        chunk_copy(c).wait()

        outs = []
        cells = []
        for u in range(per):
            j = c * per + u
            k = kind[j]
            cells.append(route[j] * nkern + k)
            outs.append(
                jnp.dot(angle[k], expand(pbuf[j], width), preferred_element_type=jnp.float32)
            )
        for cell, out in zip(cells, outs):
            y[cell] += out


def merge_kernel(
    n, y, ghi, glo, twiddle, out, xcat, own, sbuf, rbuf_r, rbuf_l, pair,
    send_sem, recv_r, recv_l, pair_send, pair_recv,
):
    tile_dev, width, double = out.shape
    rows = tile_dev * width
    nkern = ghi.shape[0] // double
    piece = rows // PIECES
    z = lax.axis_index("aperture")
    b = lax.axis_index("beam")
    has_left = z > 0
    has_right = z < n - 1

    barrier = pltpu.get_barrier_semaphore()

    @pl.when(has_left)
    def _():
        pl.semaphore_signal(barrier, inc=1, device_id={"aperture": z - 1}, device_id_type=MESH)

    @pl.when(has_right)
    def _():
        pl.semaphore_signal(barrier, inc=1, device_id={"aperture": z + 1}, device_id_type=MESH)

    pl.semaphore_signal(barrier, inc=1, device_id={"beam": 1 - b}, device_id_type=MESH)

    ahead = n - 1 - z
    near = jnp.minimum(ahead, z)
    lead = jnp.maximum(ahead, z) - near

    def dest(i):
        first = jnp.where(ahead > z, n - 1 - i, i)
        j = i - lead
        gap = near - j // 2
        later = jnp.where(j % 2 == 0, z + gap, z - gap)
        return jnp.where(i < lead, first, later)

    def span(p):
        return pl.ds(p * piece, piece)

    def send_right(d, p):
        return pltpu.make_async_remote_copy(
            src_ref=sbuf.at[d, span(p)], dst_ref=rbuf_r.at[d, span(p)],
            send_sem=send_sem.at[d, p], recv_sem=recv_r.at[d, p],
            device_id={"aperture": z + 1}, device_id_type=MESH,
        )

    def send_left(d, p):
        return pltpu.make_async_remote_copy(
            src_ref=sbuf.at[d, span(p)], dst_ref=rbuf_l.at[d, span(p)],
            send_sem=send_sem.at[d, p], recv_sem=recv_l.at[d, p],
            device_id={"aperture": z - 1}, device_id_type=MESH,
        )

    def send_pair(p):
        return pltpu.make_async_remote_copy(
            src_ref=own.at[z, span(p)], dst_ref=pair.at[span(p)],
            send_sem=pair_send.at[p], recv_sem=pair_recv.at[p],
            device_id={"beam": 1 - b}, device_id_type=MESH,
        )

    @pl.loop(0, n)
    def _(i):
        d = dest(i)
        for t in range(tile_dev):
            for k in range(nkern):
                xcat[t * width:(t + 1) * width, k * double:(k + 1) * double] = y[
                    (d * tile_dev + t) * nkern + k
                ].astype(jnp.bfloat16)
        own[d] = jnp.dot(xcat[...], ghi[...], preferred_element_type=jnp.float32) + jnp.dot(
            xcat[...], glo[...], preferred_element_type=jnp.float32
        )

        @pl.when(i == 0)
        def _():
            links = has_left.astype(jnp.int32) + has_right.astype(jnp.int32) + 1
            pl.semaphore_wait(barrier, links)

        @pl.when(jnp.logical_and(z == 0, d > z))
        def _():
            sbuf[d] = own[d].astype(jnp.bfloat16)
            for p in range(PIECES):
                send_right(d, p).start()

        @pl.when(jnp.logical_and(z == n - 1, d < z))
        def _():
            sbuf[d] = own[d].astype(jnp.bfloat16)
            for p in range(PIECES):
                send_left(d, p).start()

    @pl.when(jnp.logical_and(has_left, has_right))
    def _():
        @pl.loop(0, n - 1)
        def _(i):
            d = dest(i)

            @pl.when(d > z)
            def _():
                for p in range(PIECES):
                    send_right(d, p).wait_recv()
                    part = own[d, span(p)] + rbuf_r[d, span(p)].astype(jnp.float32)
                    sbuf[d, span(p)] = part.astype(jnp.bfloat16)
                    send_right(d, p).start()

            @pl.when(d < z)
            def _():
                for p in range(PIECES):
                    send_left(d, p).wait_recv()
                    part = own[d, span(p)] + rbuf_l[d, span(p)].astype(jnp.float32)
                    sbuf[d, span(p)] = part.astype(jnp.bfloat16)
                    send_left(d, p).start()

    for p in range(PIECES):
        @pl.when(has_left)
        def _():
            send_right(z, p).wait_recv()
            own[z, span(p)] += rbuf_r[z, span(p)].astype(jnp.float32)

        @pl.when(has_right)
        def _():
            send_left(z, p).wait_recv()
            own[z, span(p)] += rbuf_l[z, span(p)].astype(jnp.float32)

        send_pair(p).start()

    cos_all, sin_all = jnp.cos(twiddle[...]), jnp.sin(twiddle[...])
    is_even = b == 0
    sign = jnp.where(is_even, 1.0, -1.0).astype(jnp.float32)
    for p in range(PIECES):
        send_pair(p).wait_recv()
        t, base = p * piece // width, p * piece % width
        mine, other = own[z, span(p)], pair[span(p)]
        even = jnp.where(is_even, mine, other)
        odd = jnp.where(is_even, other, mine)
        cos, sin = cos_all[t:t + 1], sin_all[t:t + 1]
        odd_re, odd_im = odd[:, :width], odd[:, width:]
        out[t, base:base + piece, :width] = even[:, :width] + sign * (cos * odd_re - sin * odd_im)
        out[t, base:base + piece, width:] = even[:, width:] + sign * (cos * odd_im + sin * odd_re)

    for p in range(PIECES):
        send_pair(p).wait_send()

    @pl.loop(0, n)
    def _(d):
        @pl.when(d != z)
        def _():
            for p in range(PIECES):
                send_right(d, p).wait_send()


def per_device(polar, route, kind, filt, interp_angle, interp_range, twiddle):
    n = lax.axis_size("aperture")
    tile_dev = twiddle.shape[0]
    tiles = tile_dev * n
    _, count, width, double = polar.shape
    nkern = interp_angle.shape[0]
    cells = tiles * nkern
    rows = tile_dev * width
    resident = cells * width * double * 4 <= 16 * 2**20
    held = pltpu.VMEM if resident else jax.ShapeDtypeStruct
    vmem = pl.BlockSpec(memory_space=pltpu.VMEM)
    smem = pl.BlockSpec(memory_space=pltpu.SMEM)
    y, ghi, glo = pl.pallas_call(
        functools.partial(angle_kernel, nkern),
        out_shape=[
            held((cells, width, double), jnp.float32),
            held((nkern * double, double), jnp.bfloat16),
            held((nkern * double, double), jnp.bfloat16),
        ],
        in_specs=[smem, smem] + [pl.BlockSpec(memory_space=pl.ANY)] * 4,
        out_specs=[vmem, vmem, vmem],
        scratch_shapes=[
            pltpu.VMEM((width, double), jnp.bfloat16),
            pltpu.VMEM((nkern, width, double), jnp.bfloat16),
            pltpu.VMEM((nkern, width, double), jnp.bfloat16),
            pltpu.VMEM((count, width, double), jnp.bfloat16),
            pltpu.SemaphoreType.DMA((3,)),
            pltpu.SemaphoreType.DMA((CHUNKS,)),
        ],
        compiler_params=pltpu.CompilerParams(vmem_limit_bytes=(24 if resident else 48) * 2**20),
        name="angle",
    )(
        *[
            pltpu.with_memory_space_constraint(v, pltpu.HBM)
            for v in (route[0, :, 0], kind[0], filt[0], interp_angle, interp_range, polar[0])
        ],
    )
    if resident:
        y, ghi, glo = [pltpu.with_memory_space_constraint(v, pltpu.VMEM) for v in (y, ghi, glo)]
    merged = pl.pallas_call(
        functools.partial(merge_kernel, n),
        out_shape=jax.ShapeDtypeStruct((tile_dev, width, double), jnp.float32),
        in_specs=[vmem, vmem, vmem, vmem],
        out_specs=vmem,
        scratch_shapes=[
            pltpu.VMEM((rows, nkern * double), jnp.bfloat16),
            pltpu.VMEM((n, rows, double), jnp.float32),
            pltpu.VMEM((n, rows, double), jnp.bfloat16),
            pltpu.VMEM((n, rows, double), jnp.bfloat16),
            pltpu.VMEM((n, rows, double), jnp.bfloat16),
            pltpu.VMEM((rows, double), jnp.float32),
            pltpu.SemaphoreType.DMA((n, PIECES)),
            pltpu.SemaphoreType.DMA((n, PIECES)),
            pltpu.SemaphoreType.DMA((n, PIECES)),
            pltpu.SemaphoreType.DMA((PIECES,)),
            pltpu.SemaphoreType.DMA((PIECES,)),
        ],
        compiler_params=pltpu.CompilerParams(
            vmem_limit_bytes=(24 if resident else 58) * 2**20, collective_id=0, has_side_effects=True
        ),
        name="merge",
    )(y, ghi, glo, pltpu.with_memory_space_constraint(twiddle, pltpu.HBM))
    return merged[None]


def solution(mesh):
    return jax.shard_map(
        per_device,
        mesh=mesh,
        in_specs=(
            P(("groups", "range", "beam"), "aperture", None, None),
            P(("groups", "range", "beam"), "aperture", None),
            P(("groups", "range", "beam"), "aperture"),
            P(("groups", "range", "beam"), None, None),
            P(),
            P(),
            P("aperture", None),
        ),
        out_specs=P(("groups", "range", "beam"), "aperture", None, None),
        check_vma=False,
    )
```

```python
import functools

import jax
import jax.numpy as jnp
from jax import lax
from jax.experimental import pallas as pl
from jax.experimental.pallas import tpu as pltpu
from jax.sharding import PartitionSpec as P

MESH = pl.DeviceIdType.MESH
CHUNKS = 2
PIECES = 4


def expand(matrix, width):
    real, imag = matrix[:, :width], matrix[:, width:]
    return jnp.concatenate(
        [jnp.concatenate([real, imag], axis=1), jnp.concatenate([-imag, real], axis=1)], axis=0
    )


def angle_kernel(
    nkern, route, kind, filt_hbm, angle_hbm, rng_hbm, polar, y, ghi, glo,
    filt, angle, rng, pbuf, table_sems, sems
):
    count, width, double = pbuf.shape
    per = count // CHUNKS

    def chunk_copy(c):
        part = pl.ds(c * per, per)
        return pltpu.make_async_copy(polar.at[part], pbuf.at[part], sems.at[c])

    tables = [
        pltpu.make_async_copy(src, dst, table_sems.at[i])
        for i, (src, dst) in enumerate(((filt_hbm, filt), (rng_hbm, rng), (angle_hbm, angle)))
    ]
    for copy in tables:
        copy.start()
    for c in range(CHUNKS):
        chunk_copy(c).start()

    tables[0].wait()
    tables[1].wait()

    products = [
        jnp.dot(filt[...], expand(rng[k], width), preferred_element_type=jnp.float32)
        for k in range(nkern)
    ]
    share = y.shape[0] // nkern
    for k, g in enumerate(products):
        for cell in range(k * share, (k + 1) * share):
            y[cell] = jnp.zeros((width, double), jnp.float32)
        hi = g.astype(jnp.bfloat16)
        lo = (g - hi.astype(jnp.float32)).astype(jnp.bfloat16)
        ghi[k * double:(k + 1) * double, :] = expand(hi, width)
        glo[k * double:(k + 1) * double, :] = expand(lo, width)

    tables[2].wait()

    @pl.loop(0, CHUNKS)
    def _(c):
        chunk_copy(c).wait()

        outs = []
        cells = []
        for u in range(per):
            j = c * per + u
            k = kind[j]
            cells.append(route[j] * nkern + k)
            outs.append(
                jnp.dot(angle[k], expand(pbuf[j], width), preferred_element_type=jnp.float32)
            )
        for cell, out in zip(cells, outs):
            y[cell] += out


def merge_kernel(
    n, y, ghi, glo, twiddle, out, xcat, own, sbuf, rbuf_r, rbuf_l, pair,
    send_sem, recv_r, recv_l, pair_send, pair_recv,
):
    tile_dev, width, double = out.shape
    rows = tile_dev * width
    nkern = ghi.shape[0] // double
    piece = rows // PIECES
    z = lax.axis_index("aperture")
    b = lax.axis_index("beam")
    has_left = z > 0
    has_right = z < n - 1

    barrier = pltpu.get_barrier_semaphore()

    @pl.when(has_left)
    def _():
        pl.semaphore_signal(barrier, inc=1, device_id={"aperture": z - 1}, device_id_type=MESH)

    @pl.when(has_right)
    def _():
        pl.semaphore_signal(barrier, inc=1, device_id={"aperture": z + 1}, device_id_type=MESH)

    pl.semaphore_signal(barrier, inc=1, device_id={"beam": 1 - b}, device_id_type=MESH)

    ahead = n - 1 - z
    near = jnp.minimum(ahead, z)
    lead = jnp.maximum(ahead, z) - near

    def dest(i):
        first = jnp.where(ahead > z, n - 1 - i, i)
        j = i - lead
        gap = near - j // 2
        later = jnp.where(j % 2 == 0, z + gap, z - gap)
        return jnp.where(i < lead, first, later)

    def span(p):
        return pl.ds(p * piece, piece)

    def send_right(d, p):
        return pltpu.make_async_remote_copy(
            src_ref=sbuf.at[d, span(p)], dst_ref=rbuf_r.at[d, span(p)],
            send_sem=send_sem.at[d, p], recv_sem=recv_r.at[d, p],
            device_id={"aperture": z + 1}, device_id_type=MESH,
        )

    def send_left(d, p):
        return pltpu.make_async_remote_copy(
            src_ref=sbuf.at[d, span(p)], dst_ref=rbuf_l.at[d, span(p)],
            send_sem=send_sem.at[d, p], recv_sem=recv_l.at[d, p],
            device_id={"aperture": z - 1}, device_id_type=MESH,
        )

    def send_pair(p):
        return pltpu.make_async_remote_copy(
            src_ref=own.at[z, span(p)], dst_ref=pair.at[span(p)],
            send_sem=pair_send.at[p], recv_sem=pair_recv.at[p],
            device_id={"beam": 1 - b}, device_id_type=MESH,
        )

    @pl.loop(0, n)
    def _(i):
        d = dest(i)
        for t in range(tile_dev):
            for k in range(nkern):
                xcat[t * width:(t + 1) * width, k * double:(k + 1) * double] = y[
                    (d * tile_dev + t) * nkern + k
                ].astype(jnp.bfloat16)
        own[d] = jnp.dot(xcat[...], ghi[...], preferred_element_type=jnp.float32) + jnp.dot(
            xcat[...], glo[...], preferred_element_type=jnp.float32
        )

        @pl.when(i == 0)
        def _():
            links = has_left.astype(jnp.int32) + has_right.astype(jnp.int32) + 1
            pl.semaphore_wait(barrier, links)

        @pl.when(jnp.logical_and(z == 0, d > z))
        def _():
            sbuf[d] = own[d].astype(jnp.bfloat16)
            for p in range(PIECES):
                send_right(d, p).start()

        @pl.when(jnp.logical_and(z == n - 1, d < z))
        def _():
            sbuf[d] = own[d].astype(jnp.bfloat16)
            for p in range(PIECES):
                send_left(d, p).start()

    @pl.when(jnp.logical_and(has_left, has_right))
    def _():
        def pass_right(d, p):
            send_right(d, p).wait_recv()
            part = own[d, span(p)] + rbuf_r[d, span(p)].astype(jnp.float32)
            sbuf[d, span(p)] = part.astype(jnp.bfloat16)
            send_right(d, p).start()

        def pass_left(d, p):
            send_left(d, p).wait_recv()
            part = own[d, span(p)] + rbuf_l[d, span(p)].astype(jnp.float32)
            sbuf[d, span(p)] = part.astype(jnp.bfloat16)
            send_left(d, p).start()

        @pl.loop(0, n - 1)
        def _(i):
            @pl.when(jnp.logical_and(i < lead, ahead > z))
            def _():
                for p in range(PIECES):
                    pass_right(n - 1 - i, p)

            @pl.when(jnp.logical_and(i < lead, ahead < z))
            def _():
                for p in range(PIECES):
                    pass_left(i, p)

        @pl.loop(0, n // 2)
        def _(i):
            gap = near - i

            @pl.when(i < near)
            def _():
                for p in range(PIECES):
                    @pl.when(ahead > z)
                    def _():
                        pass_right(z + gap, p)

                    pass_left(z - gap, p)

                    @pl.when(ahead <= z)
                    def _():
                        pass_right(z + gap, p)

    for p in range(PIECES):
        @pl.when(has_left)
        def _():
            send_right(z, p).wait_recv()
            own[z, span(p)] += rbuf_r[z, span(p)].astype(jnp.float32)

        @pl.when(has_right)
        def _():
            send_left(z, p).wait_recv()
            own[z, span(p)] += rbuf_l[z, span(p)].astype(jnp.float32)

        send_pair(p).start()

    cos_all, sin_all = jnp.cos(twiddle[...]), jnp.sin(twiddle[...])
    is_even = b == 0
    sign = jnp.where(is_even, 1.0, -1.0).astype(jnp.float32)
    for p in range(PIECES):
        send_pair(p).wait_recv()
        t, base = p * piece // width, p * piece % width
        mine, other = own[z, span(p)], pair[span(p)]
        even = jnp.where(is_even, mine, other)
        odd = jnp.where(is_even, other, mine)
        cos, sin = cos_all[t:t + 1], sin_all[t:t + 1]
        odd_re, odd_im = odd[:, :width], odd[:, width:]
        out[t, base:base + piece, :width] = even[:, :width] + sign * (cos * odd_re - sin * odd_im)
        out[t, base:base + piece, width:] = even[:, width:] + sign * (cos * odd_im + sin * odd_re)

    for p in range(PIECES):
        send_pair(p).wait_send()

    @pl.loop(0, n)
    def _(d):
        @pl.when(d != z)
        def _():
            for p in range(PIECES):
                send_right(d, p).wait_send()


def per_device(polar, route, kind, filt, interp_angle, interp_range, twiddle):
    n = lax.axis_size("aperture")
    tile_dev = twiddle.shape[0]
    tiles = tile_dev * n
    _, count, width, double = polar.shape
    nkern = interp_angle.shape[0]
    cells = tiles * nkern
    rows = tile_dev * width
    resident = cells * width * double * 4 <= 16 * 2**20
    held = pltpu.VMEM if resident else jax.ShapeDtypeStruct
    vmem = pl.BlockSpec(memory_space=pltpu.VMEM)
    smem = pl.BlockSpec(memory_space=pltpu.SMEM)
    y, ghi, glo = pl.pallas_call(
        functools.partial(angle_kernel, nkern),
        out_shape=[
            held((cells, width, double), jnp.float32),
            held((nkern * double, double), jnp.bfloat16),
            held((nkern * double, double), jnp.bfloat16),
        ],
        in_specs=[smem, smem] + [pl.BlockSpec(memory_space=pl.ANY)] * 4,
        out_specs=[vmem, vmem, vmem],
        scratch_shapes=[
            pltpu.VMEM((width, double), jnp.bfloat16),
            pltpu.VMEM((nkern, width, double), jnp.bfloat16),
            pltpu.VMEM((nkern, width, double), jnp.bfloat16),
            pltpu.VMEM((count, width, double), jnp.bfloat16),
            pltpu.SemaphoreType.DMA((3,)),
            pltpu.SemaphoreType.DMA((CHUNKS,)),
        ],
        compiler_params=pltpu.CompilerParams(vmem_limit_bytes=(24 if resident else 48) * 2**20),
        name="angle",
    )(
        *[
            pltpu.with_memory_space_constraint(v, pltpu.HBM)
            for v in (route[0, :, 0], kind[0], filt[0], interp_angle, interp_range, polar[0])
        ],
    )
    if resident:
        y, ghi, glo = [pltpu.with_memory_space_constraint(v, pltpu.VMEM) for v in (y, ghi, glo)]
    merged = pl.pallas_call(
        functools.partial(merge_kernel, n),
        out_shape=jax.ShapeDtypeStruct((tile_dev, width, double), jnp.float32),
        in_specs=[vmem, vmem, vmem, vmem],
        out_specs=vmem,
        scratch_shapes=[
            pltpu.VMEM((rows, nkern * double), jnp.bfloat16),
            pltpu.VMEM((n, rows, double), jnp.float32),
            pltpu.VMEM((n, rows, double), jnp.bfloat16),
            pltpu.VMEM((n, rows, double), jnp.bfloat16),
            pltpu.VMEM((n, rows, double), jnp.bfloat16),
            pltpu.VMEM((rows, double), jnp.float32),
            pltpu.SemaphoreType.DMA((n, PIECES)),
            pltpu.SemaphoreType.DMA((n, PIECES)),
            pltpu.SemaphoreType.DMA((n, PIECES)),
            pltpu.SemaphoreType.DMA((PIECES,)),
            pltpu.SemaphoreType.DMA((PIECES,)),
        ],
        compiler_params=pltpu.CompilerParams(
            vmem_limit_bytes=(24 if resident else 58) * 2**20, collective_id=0, has_side_effects=True
        ),
        name="merge",
    )(y, ghi, glo, pltpu.with_memory_space_constraint(twiddle, pltpu.HBM))
    return merged[None]


def solution(mesh):
    return jax.shard_map(
        per_device,
        mesh=mesh,
        in_specs=(
            P(("groups", "range", "beam"), "aperture", None, None),
            P(("groups", "range", "beam"), "aperture", None),
            P(("groups", "range", "beam"), "aperture"),
            P(("groups", "range", "beam"), None, None),
            P(),
            P(),
            P("aperture", None),
        ),
        out_specs=P(("groups", "range", "beam"), "aperture", None, None),
        check_vma=False,
    )
```

```python
import functools

import jax
import jax.numpy as jnp
from jax import lax
from jax.experimental import pallas as pl
from jax.experimental.pallas import tpu as pltpu
from jax.sharding import PartitionSpec as P

MESH = pl.DeviceIdType.MESH
CHUNKS = 2
PIECES = 4


def expand(matrix, width):
    real, imag = matrix[:, :width], matrix[:, width:]
    return jnp.concatenate(
        [jnp.concatenate([real, imag], axis=1), jnp.concatenate([-imag, real], axis=1)], axis=0
    )


def angle_kernel(
    nkern, route, kind, filt_hbm, angle_hbm, rng_hbm, polar, y, ghi, glo,
    filt, angle, rng, pbuf, table_sems, sems
):
    count, width, double = pbuf.shape
    per = count // CHUNKS

    def chunk_copy(c):
        part = pl.ds(c * per, per)
        return pltpu.make_async_copy(polar.at[part], pbuf.at[part], sems.at[c])

    tables = [
        pltpu.make_async_copy(src, dst, table_sems.at[i])
        for i, (src, dst) in enumerate(((filt_hbm, filt), (rng_hbm, rng), (angle_hbm, angle)))
    ]
    for copy in tables:
        copy.start()
    for c in range(CHUNKS):
        chunk_copy(c).start()

    tables[0].wait()
    tables[1].wait()

    products = [
        jnp.dot(filt[...], expand(rng[k], width), preferred_element_type=jnp.float32)
        for k in range(nkern)
    ]
    share = y.shape[0] // nkern
    for k, g in enumerate(products):
        for cell in range(k * share, (k + 1) * share):
            y[cell] = jnp.zeros((width, double), jnp.float32)
        hi = g.astype(jnp.bfloat16)
        lo = (g - hi.astype(jnp.float32)).astype(jnp.bfloat16)
        ghi[k * double:(k + 1) * double, :] = expand(hi, width)
        glo[k * double:(k + 1) * double, :] = expand(lo, width)

    tables[2].wait()

    @pl.loop(0, CHUNKS)
    def _(c):
        chunk_copy(c).wait()

        outs = []
        cells = []
        for u in range(per):
            j = c * per + u
            k = kind[j]
            cells.append(route[j] * nkern + k)
            outs.append(
                jnp.dot(angle[k], expand(pbuf[j], width), preferred_element_type=jnp.float32)
            )
        for cell, out in zip(cells, outs):
            y[cell] += out


def merge_kernel(
    n, y, ghi, glo, twiddle, out, xcat, own, sbuf, rbuf_r, rbuf_l, pair,
    send_sem, recv_r, recv_l, pair_send, pair_recv,
):
    tile_dev, width, double = out.shape
    rows = tile_dev * width
    nkern = ghi.shape[0] // double
    piece = rows // PIECES
    z = lax.axis_index("aperture")
    b = lax.axis_index("beam")
    has_left = z > 0
    has_right = z < n - 1

    barrier = pltpu.get_barrier_semaphore()

    @pl.when(has_left)
    def _():
        pl.semaphore_signal(barrier, inc=1, device_id={"aperture": z - 1}, device_id_type=MESH)

    @pl.when(has_right)
    def _():
        pl.semaphore_signal(barrier, inc=1, device_id={"aperture": z + 1}, device_id_type=MESH)

    pl.semaphore_signal(barrier, inc=1, device_id={"beam": 1 - b}, device_id_type=MESH)

    ahead = n - 1 - z
    near = jnp.minimum(ahead, z)
    lead = jnp.maximum(ahead, z) - near

    def dest(i):
        first = jnp.where(ahead > z, n - 1 - i, i)
        j = i - lead
        gap = near - j // 2
        later = jnp.where(j % 2 == 0, z + gap, z - gap)
        return jnp.where(i < lead, first, later)

    def span(p):
        return pl.ds(p * piece, piece)

    def send_right(d, p):
        return pltpu.make_async_remote_copy(
            src_ref=sbuf.at[d, span(p)], dst_ref=rbuf_r.at[d, span(p)],
            send_sem=send_sem.at[d, p], recv_sem=recv_r.at[d, p],
            device_id={"aperture": z + 1}, device_id_type=MESH,
        )

    def send_left(d, p):
        return pltpu.make_async_remote_copy(
            src_ref=sbuf.at[d, span(p)], dst_ref=rbuf_l.at[d, span(p)],
            send_sem=send_sem.at[d, p], recv_sem=recv_l.at[d, p],
            device_id={"aperture": z - 1}, device_id_type=MESH,
        )

    def send_pair(p):
        return pltpu.make_async_remote_copy(
            src_ref=own.at[z, span(p)], dst_ref=pair.at[span(p)],
            send_sem=pair_send.at[p], recv_sem=pair_recv.at[p],
            device_id={"beam": 1 - b}, device_id_type=MESH,
        )

    def gather_item(d):
        for t in range(tile_dev):
            for k in range(nkern):
                xcat[t * width:(t + 1) * width, k * double:(k + 1) * double] = y[
                    (d * tile_dev + t) * nkern + k
                ].astype(jnp.bfloat16)
        own[d] = jnp.dot(xcat[...], ghi[...], preferred_element_type=jnp.float32) + jnp.dot(
            xcat[...], glo[...], preferred_element_type=jnp.float32
        )

    @pl.loop(0, n - 1)
    def _(i):
        d = dest(i)
        gather_item(d)

        @pl.when(i == 0)
        def _():
            links = has_left.astype(jnp.int32) + has_right.astype(jnp.int32) + 1
            pl.semaphore_wait(barrier, links)

        @pl.when(jnp.logical_and(z == 0, d > z))
        def _():
            sbuf[d] = own[d].astype(jnp.bfloat16)
            for p in range(PIECES):
                send_right(d, p).start()

        @pl.when(jnp.logical_and(z == n - 1, d < z))
        def _():
            sbuf[d] = own[d].astype(jnp.bfloat16)
            for p in range(PIECES):
                send_left(d, p).start()

    @pl.when(jnp.logical_and(has_left, has_right))
    def _():
        def pass_right(d, p):
            send_right(d, p).wait_recv()
            part = own[d, span(p)] + rbuf_r[d, span(p)].astype(jnp.float32)
            sbuf[d, span(p)] = part.astype(jnp.bfloat16)
            send_right(d, p).start()

        def pass_left(d, p):
            send_left(d, p).wait_recv()
            part = own[d, span(p)] + rbuf_l[d, span(p)].astype(jnp.float32)
            sbuf[d, span(p)] = part.astype(jnp.bfloat16)
            send_left(d, p).start()

        @pl.loop(0, n - 1)
        def _(i):
            @pl.when(jnp.logical_and(i < lead, ahead > z))
            def _():
                for p in range(PIECES):
                    pass_right(n - 1 - i, p)

            @pl.when(jnp.logical_and(i < lead, ahead < z))
            def _():
                for p in range(PIECES):
                    pass_left(i, p)

        @pl.loop(0, n // 2)
        def _(i):
            gap = near - i

            @pl.when(i < near)
            def _():
                for p in range(PIECES):
                    @pl.when(ahead > z)
                    def _():
                        pass_right(z + gap, p)

                    pass_left(z - gap, p)

                    @pl.when(ahead <= z)
                    def _():
                        pass_right(z + gap, p)

    gather_item(z)

    for p in range(PIECES):
        @pl.when(has_left)
        def _():
            send_right(z, p).wait_recv()
            own[z, span(p)] += rbuf_r[z, span(p)].astype(jnp.float32)

        @pl.when(has_right)
        def _():
            send_left(z, p).wait_recv()
            own[z, span(p)] += rbuf_l[z, span(p)].astype(jnp.float32)

        send_pair(p).start()

    cos_all, sin_all = jnp.cos(twiddle[...]), jnp.sin(twiddle[...])
    is_even = b == 0
    sign = jnp.where(is_even, 1.0, -1.0).astype(jnp.float32)
    for p in range(PIECES):
        send_pair(p).wait_recv()
        t, base = p * piece // width, p * piece % width
        mine, other = own[z, span(p)], pair[span(p)]
        even = jnp.where(is_even, mine, other)
        odd = jnp.where(is_even, other, mine)
        cos, sin = cos_all[t:t + 1], sin_all[t:t + 1]
        odd_re, odd_im = odd[:, :width], odd[:, width:]
        out[t, base:base + piece, :width] = even[:, :width] + sign * (cos * odd_re - sin * odd_im)
        out[t, base:base + piece, width:] = even[:, width:] + sign * (cos * odd_im + sin * odd_re)

    for p in range(PIECES):
        send_pair(p).wait_send()

    @pl.loop(0, n)
    def _(d):
        @pl.when(d != z)
        def _():
            for p in range(PIECES):
                send_right(d, p).wait_send()


def per_device(polar, route, kind, filt, interp_angle, interp_range, twiddle):
    n = lax.axis_size("aperture")
    tile_dev = twiddle.shape[0]
    tiles = tile_dev * n
    _, count, width, double = polar.shape
    nkern = interp_angle.shape[0]
    cells = tiles * nkern
    rows = tile_dev * width
    resident = cells * width * double * 4 <= 16 * 2**20
    held = pltpu.VMEM if resident else jax.ShapeDtypeStruct
    vmem = pl.BlockSpec(memory_space=pltpu.VMEM)
    smem = pl.BlockSpec(memory_space=pltpu.SMEM)
    y, ghi, glo = pl.pallas_call(
        functools.partial(angle_kernel, nkern),
        out_shape=[
            held((cells, width, double), jnp.float32),
            held((nkern * double, double), jnp.bfloat16),
            held((nkern * double, double), jnp.bfloat16),
        ],
        in_specs=[smem, smem] + [pl.BlockSpec(memory_space=pl.ANY)] * 4,
        out_specs=[vmem, vmem, vmem],
        scratch_shapes=[
            pltpu.VMEM((width, double), jnp.bfloat16),
            pltpu.VMEM((nkern, width, double), jnp.bfloat16),
            pltpu.VMEM((nkern, width, double), jnp.bfloat16),
            pltpu.VMEM((count, width, double), jnp.bfloat16),
            pltpu.SemaphoreType.DMA((3,)),
            pltpu.SemaphoreType.DMA((CHUNKS,)),
        ],
        compiler_params=pltpu.CompilerParams(vmem_limit_bytes=(24 if resident else 48) * 2**20),
        name="angle",
    )(
        *[
            pltpu.with_memory_space_constraint(v, pltpu.HBM)
            for v in (route[0, :, 0], kind[0], filt[0], interp_angle, interp_range, polar[0])
        ],
    )
    if resident:
        y, ghi, glo = [pltpu.with_memory_space_constraint(v, pltpu.VMEM) for v in (y, ghi, glo)]
    merged = pl.pallas_call(
        functools.partial(merge_kernel, n),
        out_shape=jax.ShapeDtypeStruct((tile_dev, width, double), jnp.float32),
        in_specs=[vmem, vmem, vmem, vmem],
        out_specs=vmem,
        scratch_shapes=[
            pltpu.VMEM((rows, nkern * double), jnp.bfloat16),
            pltpu.VMEM((n, rows, double), jnp.float32),
            pltpu.VMEM((n, rows, double), jnp.bfloat16),
            pltpu.VMEM((n, rows, double), jnp.bfloat16),
            pltpu.VMEM((n, rows, double), jnp.bfloat16),
            pltpu.VMEM((rows, double), jnp.float32),
            pltpu.SemaphoreType.DMA((n, PIECES)),
            pltpu.SemaphoreType.DMA((n, PIECES)),
            pltpu.SemaphoreType.DMA((n, PIECES)),
            pltpu.SemaphoreType.DMA((PIECES,)),
            pltpu.SemaphoreType.DMA((PIECES,)),
        ],
        compiler_params=pltpu.CompilerParams(
            vmem_limit_bytes=(24 if resident else 58) * 2**20, collective_id=0, has_side_effects=True
        ),
        name="merge",
    )(y, ghi, glo, pltpu.with_memory_space_constraint(twiddle, pltpu.HBM))
    return merged[None]


def solution(mesh):
    return jax.shard_map(
        per_device,
        mesh=mesh,
        in_specs=(
            P(("groups", "range", "beam"), "aperture", None, None),
            P(("groups", "range", "beam"), "aperture", None),
            P(("groups", "range", "beam"), "aperture"),
            P(("groups", "range", "beam"), None, None),
            P(),
            P(),
            P("aperture", None),
        ),
        out_specs=P(("groups", "range", "beam"), "aperture", None, None),
        check_vma=False,
    )
```
